256 devices in a mesh: dp: 4 (over x), expert: 64 (over y, z, core).
Axes of the slice: x: 4, y: 4, z: 8, core: 2. Of those that a mesh axis runs over, the one named last changes fastest.
Arguments:
- tokens: bfloat16 [8192, 7168], P('expert', 'dp'), may hold values from -6 to 6
- gate_up: bfloat16 [64, 7168, 2, 1024], P('expert', 'dp'), may hold values from -0.0625 to 0.0625
- down: bfloat16 [64, 1024, 7168], P('expert', None, 'dp'), may hold values from -0.1875 to 0.1875
- route_ids: int32 [8192, 8], P('expert'), may hold values from 0 to 63, all different within a row; in each aligned block of 128 rows (0 to 127, 128 to 255, ...) at most 18 rows name the same one
- route_weight: bfloat16 [8192, 8], P('expert'), may hold values from 0.099609375 to 0.59765625
- swap_flags: int32 [64], replicated, may hold values from 0 to 1, as said below
Outputs:
- mixed: bfloat16 [8192, 7168], P('expert', 'dp')
The draws below stay inside these ranges and needn't reach their ends.
Inputs may be any that keep to these rules, and one draw needn't show every extreme that they name: `route_ids`: each row names 8 different slots; among the 128 rows of one device no slot is named by more than 18 rows, a bound that some block reaches. swap_flags[j] equals swap_flags[j + 32] for every j below 32.
All inputs are finite; a program needn't handle non-finite values.
Results may differ from the reference program's by a relative error of at most 0.024.
Values may be sent and summed in bfloat16 or wider, within the bound.
No kernel may reach another device: no remote copies, remote signals or barrier semaphores. Data moves between devices by JAX's collectives and lax.ppermute only.
A program may use at most 128 MiB of HBM per device.

```python
import math
import jax
import jax.numpy as jnp
import numpy as np
from jax import lax

D = 7168
H = 1024
TOP = 8
TOK_DEV = 128
EXPERTS = 64
CAP = 18
TOKENS = 8192
N_DP = 4
N_EXPERT = 64


def draw_swap_flags(key, part):
    key = jax.random.fold_in(key, 7)
    first_half = jax.random.randint(key, (EXPERTS // 2,), 0, 2, dtype=jnp.int32)
    return jnp.concatenate([first_half, first_half])


def levels(own_key, extent, cuts, smallest, largest):
    def one(position, blocks):
        steps = jax.random.uniform(jax.random.fold_in(jax.random.fold_in(own_key, 6), position), (blocks,), jnp.float32, smallest / len(cuts), largest / len(cuts))
        return jnp.repeat(jnp.exp(steps), extent[position] // blocks).reshape((-1,) + (1,) * (len(extent) - position - 1))

    level = one(*cuts[0])
    for cut in cuts[1:]:
        level = level * one(*cut)
    return level


def routed_block(rng, own, number, rows, amount, top, bound, lean):
    ranking = jax.random.permutation(rng, amount)
    crowded, usual = shares(amount, rows * top, bound, lean, True), shares(amount, rows * top, bound, lean, False)
    places = jnp.arange(amount)

    def named(lengths, turn):
        used = int((lengths > 0).sum())
        fixed = max(1, used // 4)
        passed = fixed + (places - fixed + turn * (used - fixed)) % max(1, amount - fixed)
        return jnp.zeros((amount,), jnp.int32).at[ranking[jnp.where(places < fixed, places, passed)]].set(jnp.asarray(lengths, jnp.int32))

    lengths = jnp.where(number % 4 == 0, named(crowded, number // 4), named(usual, number - number // 4 - 1))
    mixed = jax.random.permutation(jax.random.fold_in(own, 3), amount)
    donor, taker = mixed[0:amount // 2 * 2:2], mixed[1:amount // 2 * 2:2]
    margin = jnp.minimum(lengths[donor] - 1, bound - lengths[taker]) // 2
    margin = jnp.where((donor == ranking[0]) | (taker == ranking[0]) | (lengths[taker] == 0), 0, jnp.maximum(margin, 0))
    passed = jax.random.randint(jax.random.fold_in(own, 4), (amount // 2,), 0, 1 << 20) % (margin + 1)
    lengths = lengths.at[donor].add(-passed).at[taker].add(passed)
    members = jnp.searchsorted(jnp.cumsum(lengths), jnp.arange(rows * top), side="right").astype(jnp.int32)
    grid = members.reshape(top, rows).T
    grid = grid[jax.random.permutation(jax.random.fold_in(own, 1), rows)]
    turn = jax.random.randint(jax.random.fold_in(own, 2), (rows, 1), 0, top)
    return jnp.take_along_axis(grid, (jnp.arange(top)[None, :] + turn) % top, axis=1)


def shares(count, total, most, skew, full):
    portions = [(1 << 20) // math.isqrt(rank ** skew) + 1 for rank in range(1, count + 1)]
    largest = most if full else min(most, max(-(-total // count), total * portions[0] // sum(portions)))
    least = 1 if total - largest >= count - 1 else 0
    given, rest = [largest] + [least] * (count - 1), total - largest - least * (count - 1)
    while rest > 0:
        free = [i for i in range(1, count) if given[i] < largest] or [i for i in range(1, count) if given[i] < most]
        whole, budget = sum([portions[i] for i in free]), rest
        for i in free:
            more = min(most - given[i], max(1, budget * portions[i] // whole), rest)
            given[i] = given[i] + more
            rest = rest - more
    return np.array(given)


def bell_draw(key, extent, scale, reach, pieces=(), held_as=jnp.bfloat16):
    gain = levels(key, extent, pieces, -0.22, 0.18) if pieces else 1.0
    array = jax.random.normal(key, extent, jnp.float32) * scale * gain
    return jnp.minimum(jnp.maximum(array, -reach), reach).astype(held_as)


def setup_inputs(seed: int = 0) -> dict:
    keys = jax.random.split(jax.random.key(seed), 7)
    tokens = bell_draw(keys[0], (TOKENS, D), 1.0, 6.0, ((0, 64), (1, 4)))
    gate_up = bell_draw(keys[1], (EXPERTS, D, 2, H), D ** -0.5, 0.0625, ((0, 64), (1, 4)))
    down = bell_draw(keys[2], (EXPERTS, H, D), H ** -0.5, 0.1875, ((0, 64), (2, 4)))
    route_ids_keys = jax.random.split(jax.random.fold_in(keys[3], 1), TOKENS // TOK_DEV)
    route_ids_turns = jax.random.permutation(jax.random.fold_in(keys[3], 3), TOKENS // TOK_DEV)
    route_ids = jax.vmap(lambda own, number: routed_block(jax.random.fold_in(keys[3], 2), own, number, TOK_DEV, EXPERTS, TOP, CAP, 2))(route_ids_keys, route_ids_turns).reshape((TOKENS, TOP))
    route_weight = jnp.clip(0.099609375 + 0.49804688 * jax.random.uniform(keys[4], (TOKENS, TOP), jnp.float32) ** levels(keys[4], (TOKENS, TOP), ((0, 64),), -0.2, 0.2), 0.099609375, 0.59765625).astype(jnp.bfloat16)
    swap_flags = draw_swap_flags(jax.random.fold_in(keys[6], 71), 0)
    return dict(tokens=tokens, gate_up=gate_up, down=down, route_ids=route_ids, route_weight=route_weight, swap_flags=swap_flags)


def reference(tokens, gate_up, down, route_ids, route_weight, swap_flags):
    experts = gate_up.shape[0]
    half_axis = experts // 2
    total_rows, model_width = tokens.shape
    block_width = model_width // N_DP
    hidden_units = down.shape[1]
    slot_ids = jnp.arange(experts, dtype=jnp.int32)
    source_slot = jnp.where(swap_flags == 1, (slot_ids + half_axis) % experts, slot_ids).astype(jnp.int32)
    flat_ids = source_slot[route_ids.reshape(-1)].astype(jnp.int32)
    pair_count = flat_ids.shape[0]
    onehot = (flat_ids[:, None] == slot_ids[None, :]).astype(jnp.int32)
    slot_rank = (jnp.sum(jnp.cumsum(onehot, axis=0) * onehot, axis=1) - 1).astype(jnp.int32)
    buffer_depth = N_EXPERT * CAP
    slot_table = jnp.full((experts, buffer_depth), pair_count, jnp.int32)
    slot_table = slot_table.at[flat_ids, slot_rank].set(jnp.arange(pair_count, dtype=jnp.int32))
    weights_flat = jnp.concatenate([route_weight.reshape(-1).astype(jnp.float32), jnp.zeros((1,), jnp.float32)])
    padded = jnp.concatenate([tokens, jnp.zeros((1, model_width), tokens.dtype)], axis=0)

    def one_expert(running, expert_index):
        chosen = slot_table[expert_index]
        is_valid = chosen < pair_count
        gather_rows = jnp.where(is_valid, chosen // TOP, total_rows).astype(jnp.int32)
        row_block = padded[gather_rows]
        expert_gu = gate_up[expert_index]
        expert_dn = down[expert_index]
        summed = jnp.zeros((buffer_depth, 2 * hidden_units), jnp.float32)
        for block_index in range(N_DP):
            low = block_index * block_width
            part_sum = jnp.dot(row_block[:, low:low + block_width],
                               expert_gu[low:low + block_width].reshape(block_width, 2 * hidden_units),
                               preferred_element_type=jnp.float32)
            summed = summed + lax.optimization_barrier(part_sum.astype(jnp.bfloat16)).astype(jnp.float32)
        summed = summed.reshape(buffer_depth, 2, hidden_units)
        hidden = (jax.nn.silu(summed[:, 0]) * summed[:, 1]).astype(jnp.bfloat16)
        out_rows = jnp.dot(hidden, expert_dn, preferred_element_type=jnp.float32).astype(jnp.bfloat16)
        weight_col = weights_flat[chosen]
        contrib = lax.optimization_barrier(out_rows).astype(jnp.float32) * weight_col[:, None]
        running = running.at[gather_rows].add(contrib)
        return running, None

    running = jnp.zeros((total_rows + 1, model_width), jnp.float32)
    running, _ = lax.scan(one_expert, running, slot_ids)
    return running[:total_rows].astype(jnp.bfloat16)
```

```python
import jax
import jax.numpy as jnp
from jax import lax
from jax.sharding import PartitionSpec as P

TOP = 8


def body(tokens, gate_up, down, route_ids, route_weight, swap_flags):
    members = lax.axis_size("expert")
    half_axis = members // 2
    tok_rows, feat_width = tokens.shape
    hidden_units = down.shape[1]
    capacity = min(tok_rows, 9 * tok_rows * TOP // (8 * members))
    use_gu = gate_up[0]
    use_dn = down[0]
    slot_ids = jnp.arange(members, dtype=jnp.int32)
    source_slot = jnp.where(swap_flags == 1, (slot_ids + half_axis) % members, slot_ids)
    new_ids = route_ids.reshape(-1)
    flat_ids = jnp.sum(jnp.where(new_ids[:, None] == slot_ids[None, :], source_slot[None, :], 0), axis=1)
    onehot = (flat_ids[:, None] == slot_ids[None, :]).astype(jnp.int32)
    slot_rank = jnp.sum(jnp.cumsum(onehot, axis=0) * onehot, axis=1) - 1
    position = flat_ids * capacity + slot_rank
    pair_row = jnp.arange(flat_ids.shape[0], dtype=jnp.int32) // TOP
    source_row = jnp.full((members * capacity,), tok_rows, jnp.int32).at[position].set(pair_row)
    padded = jnp.concatenate([tokens, jnp.zeros((1, feat_width), tokens.dtype)], axis=0)
    outgoing = padded[source_row].reshape(members, capacity, feat_width)
    flat_gu = use_gu.reshape(feat_width, 2 * hidden_units)
    received = lax.all_to_all(outgoing, "expert", split_axis=0, concat_axis=0, tiled=True)
    senders, item_count, _ = received.shape
    row_block = received.reshape(senders * item_count, feat_width)
    partial_value = jnp.dot(row_block, flat_gu, preferred_element_type=jnp.float32).reshape(
        -1, 2, hidden_units
    )
    summed = lax.psum(partial_value.astype(jnp.bfloat16), "dp").astype(jnp.float32)
    hidden = (jax.nn.silu(summed[:, 0]) * summed[:, 1]).astype(jnp.bfloat16)
    result = jnp.dot(hidden, use_dn, preferred_element_type=jnp.float32).astype(jnp.bfloat16)
    result = result.reshape(senders, item_count, feat_width)
    returned_rows = lax.all_to_all(result, "expert", split_axis=0, concat_axis=0, tiled=True)
    picked = returned_rows.reshape(members * capacity, feat_width)[position]
    picked = picked.reshape(tok_rows, TOP, feat_width).astype(jnp.float32)
    mixed = jnp.sum(picked * route_weight.astype(jnp.float32)[..., None], axis=1)
    return mixed.astype(jnp.bfloat16)


def solution(mesh):
    return jax.shard_map(
        body,
        mesh=mesh,
        in_specs=(
            P("expert", "dp"),
            P("expert", "dp", None, None),
            P("expert", None, "dp"),
            P("expert", None),
            P("expert", None),
            P(),
        ),
        out_specs=P("expert", "dp"),
        check_vma=False,
    )
```

```python
import jax
import jax.numpy as jnp
from jax import lax
from jax.sharding import Mesh, PartitionSpec as P

N_Y, N_Z, N_C = 4, 8, 2
N_YC = N_Y * N_C
CHUNKS = 2
BF16 = jnp.bfloat16
F32 = jnp.float32


def routing_table(route_ids, route_weight, swap_flags):
    tok_rows = route_ids.shape[0]
    experts = swap_flags.shape[0]
    half = experts // 2
    hit = route_ids[:, :, None] == jnp.arange(experts, dtype=jnp.int32)
    named = jnp.any(hit, axis=1).astype(F32)
    weight = jnp.sum(jnp.where(hit, route_weight.astype(F32)[:, :, None], 0.0), axis=1)
    swapped = swap_flags[None, :] == 1
    named = jnp.where(swapped, jnp.roll(named, half, axis=1), named)
    weight = jnp.where(swapped, jnp.roll(weight, half, axis=1), weight)
    upto = jnp.tril(jnp.ones((tok_rows, tok_rows), BF16))
    place = jnp.dot(upto, named.astype(BF16), preferred_element_type=F32) * named
    return jnp.concatenate([place, weight], axis=1).astype(BF16)


def body(tokens, gate_up, down, route_ids, route_weight, swap_flags):
    tok_rows, feat_width = tokens.shape
    experts = swap_flags.shape[0]
    hidden_units = down.shape[1]
    top = route_ids.shape[1]
    capacity = min(tok_rows, 9 * tok_rows * top // (8 * experts))
    flat_gu = gate_up[0].reshape(feat_width, 2 * hidden_units)
    dn = down[0]
    my_z = lax.axis_index("z")

    table = routing_table(route_ids, route_weight, swap_flags)
    wide = jnp.concatenate([tokens, table], axis=1)
    column = lax.all_gather(wide, "z", axis=0, tiled=True)
    dest = jnp.arange(N_YC, dtype=jnp.int32)
    plane = ((dest // N_C) * N_Z + my_z) * N_C + dest % N_C
    pick = (jnp.arange(experts, dtype=jnp.int32)[:, None] == plane[None, :]).astype(BF16)
    places = jnp.dot(column[:, feat_width:feat_width + experts], pick, preferred_element_type=F32)
    weights = jnp.dot(column[:, feat_width + experts:], pick, preferred_element_type=F32)

    per = N_Z // CHUNKS
    rows = per * capacity
    toks = per * tok_rows
    sums = []
    row = jnp.arange(rows, dtype=jnp.int32)
    tok = jnp.arange(toks, dtype=jnp.int32)
    same = (row // capacity)[:, None] == (tok // tok_rows)[None, :]
    want = (row % capacity + 1).astype(F32)
    for chunk in range(CHUNKS):
        part = slice(chunk * toks, (chunk + 1) * toks)
        p, w = places[part].T, weights[part].T
        chosen = same[None] & (p[:, None, :] == want[None, :, None])
        gather = chosen.astype(BF16).reshape(N_YC * rows, toks)
        scatter = jnp.where(chosen, w[:, None, :], 0.0).astype(BF16).reshape(N_YC * rows, toks)
        outgoing = jnp.dot(gather, column[part, :feat_width], preferred_element_type=F32).astype(BF16)
        received = lax.all_to_all(outgoing.reshape(N_YC, rows, feat_width), ("y", "c"), 0, 0, tiled=True)
        received = received.reshape(N_YC * rows, feat_width)
        partial = jnp.dot(received, flat_gu, preferred_element_type=F32).astype(BF16)
        pre = lax.psum_scatter(partial, "x", scatter_dimension=0, tiled=True).astype(F32)
        hidden = (jax.nn.silu(pre[:, :hidden_units]) * pre[:, hidden_units:]).astype(BF16)
        hidden = lax.all_gather(hidden, "x", axis=0, tiled=True)
        result = jnp.dot(hidden, dn, preferred_element_type=F32).astype(BF16)
        back = lax.all_to_all(result.reshape(N_YC, rows, feat_width), ("y", "c"), 0, 0, tiled=True)
        back = back.reshape(N_YC * rows, feat_width)
        sums.append(lax.dot_general(scatter, back, (((0,), (0,)), ((), ())), preferred_element_type=F32).astype(BF16))
    return lax.psum_scatter(jnp.concatenate(sums, axis=0), "z", scatter_dimension=0, tiled=True)


def solution(mesh):
    grid = Mesh(mesh.devices.reshape(mesh.devices.shape[0], N_Y, N_Z, N_C), ("x", "y", "z", "c"))
    expert = ("y", "z", "c")
    return jax.shard_map(
        body,
        mesh=grid,
        in_specs=(
            P(expert, "x"),
            P(expert, "x", None, None),
            P(expert, None, "x"),
            P(expert, None),
            P(expert, None),
            P(),
        ),
        out_specs=P(expert, "x"),
        check_vma=False,
    )
```

```python
import jax
import jax.numpy as jnp
from jax import lax
from jax.experimental import pallas as pl
from jax.sharding import Mesh, PartitionSpec as P

N_X, N_Y, N_Z, N_C = 4, 4, 8, 2
N_YC = N_Y * N_C
GROUPS = ((0, 1, -1, 2), (-2, 3, -3, 4))
HALVES = 2
RS_SC = False
BF16 = jnp.bfloat16
F32 = jnp.float32


def shift(block, axis, distance):
    size = lax.axis_size(axis)
    return lax.ppermute(block, axis, [(i, (i + distance) % size) for i in range(size)])


def after(value, *others):
    anywhere = pl.BlockSpec(memory_space=pl.ANY)
    return pl.pallas_call(
        lambda *refs: None,
        out_shape=jax.ShapeDtypeStruct(value.shape, value.dtype),
        in_specs=[anywhere] * (1 + len(others)),
        out_specs=anywhere,
        input_output_aliases={0: 0},
        cost_estimate=pl.CostEstimate(flops=0, bytes_accessed=0, transcendentals=0),
        name="after",
    )(value, *others)


def routing_table(route_ids, route_weight, swap_flags):
    tok_rows = route_ids.shape[0]
    experts = swap_flags.shape[0]
    half = experts // 2
    hit = route_ids[:, :, None] == jnp.arange(experts, dtype=jnp.int32)
    named = jnp.any(hit, axis=1).astype(F32)
    weight = jnp.sum(jnp.where(hit, route_weight.astype(F32)[:, :, None], 0.0), axis=1)
    swapped = swap_flags[None, :] == 1
    named = jnp.where(swapped, jnp.roll(named, half, axis=1), named)
    weight = jnp.where(swapped, jnp.roll(weight, half, axis=1), weight)
    upto = jnp.tril(jnp.ones((tok_rows, tok_rows), BF16))
    place = jnp.dot(upto, named.astype(BF16), preferred_element_type=F32) * named
    return jnp.concatenate([place, weight], axis=1).astype(BF16)


def scatter_z(part):
    far = N_Z // 2
    cut = part(far).shape[0] // 2
    down = part(far)[:cut]
    up = part(far)[cut:]
    down, up = shift(down, "z", -1), shift(up, "z", 1)
    down = jnp.concatenate([part(far - 1)[:cut] + down, part(far - 1)[cut:]], axis=0)
    up = jnp.concatenate([part(1 - far)[:cut], part(1 - far)[cut:] + up], axis=0)
    for step in range(far - 2, 0, -1):
        down = part(step) + shift(down, "z", -1)
        up = part(-step) + shift(up, "z", 1)
    mine = part(0).astype(F32) + shift(down, "z", -1).astype(F32) + shift(up, "z", 1).astype(F32)
    return mine.astype(BF16)


def body(tokens, gate_up, down, route_ids, route_weight, swap_flags):
    tok_rows, feat_width = tokens.shape
    experts = swap_flags.shape[0]
    hidden_units = down.shape[1]
    top = route_ids.shape[1]
    capacity = min(tok_rows, 9 * tok_rows * top // (8 * experts))
    flat_gu = gate_up[0].reshape(feat_width, 2 * hidden_units)
    dn = down[0]
    my_x, my_z = lax.axis_index("x"), lax.axis_index("z")

    table = routing_table(route_ids, route_weight, swap_flags)
    dest = jnp.arange(N_YC, dtype=jnp.int32)
    plane = ((dest // N_C) * N_Z + my_z) * N_C + dest % N_C
    pick = (jnp.arange(experts, dtype=jnp.int32)[:, None] == plane[None, :]).astype(BF16)

    def pick_rows(blocks, group):
        count = len(group)
        rows = -(-count * capacity // 8) * 8
        toks = count * tok_rows
        row = jnp.arange(rows, dtype=jnp.int32)
        tok = jnp.arange(toks, dtype=jnp.int32)
        same = (row // capacity)[:, None] == (tok // tok_rows)[None, :]
        want = (row % capacity + 1).astype(F32)
        column = jnp.concatenate([blocks[d] for d in group], axis=0)
        places = jnp.dot(column[:, feat_width:feat_width + experts], pick, preferred_element_type=F32).T
        weights = jnp.dot(column[:, feat_width + experts:], pick, preferred_element_type=F32).T
        chosen = same[None] & (places[:, None, :] == want[None, :, None])
        gather = chosen.astype(BF16).reshape(N_YC * rows, toks)
        scatter = jnp.where(chosen, weights[:, None, :], 0.0).astype(BF16).reshape(N_YC * rows, toks)
        outgoing = jnp.dot(gather, column[:, :feat_width], preferred_element_type=F32).astype(BF16)
        return outgoing, scatter

    def cross(rows):
        blocks = rows.reshape(N_YC, rows.shape[0] // N_YC, feat_width)
        return lax.all_to_all(blocks, ("y", "c"), 0, 0, tiled=True).reshape(rows.shape)

    def up_projection(rows):
        return jnp.dot(rows, flat_gu, preferred_element_type=F32).astype(BF16)

    def scatter_x(partial):
        if RS_SC:
            return lax.psum_scatter(partial, "x", scatter_dimension=0, tiled=True).astype(F32)
        share = partial.shape[0] // N_X
        total = None
        for distance in (2, 1, 3, 0):
            piece = lax.dynamic_slice_in_dim(partial, lax.rem(my_x + distance, N_X) * share, share, axis=0)
            if distance:
                piece = shift(piece, "x", distance)
            total = piece.astype(F32) if total is None else total + piece.astype(F32)
        return total

    def activation(pre):
        return (jax.nn.silu(pre[:, :hidden_units]) * pre[:, hidden_units:]).astype(BF16)

    def gather_x(block):
        rows = block.shape[0]
        whole = jnp.zeros((N_X * rows, hidden_units), BF16)
        for distance in (0, 1, 3, 2):
            piece = shift(block, "x", distance) if distance else block
            whole = lax.dynamic_update_slice(whole, piece, (lax.rem(my_x + N_X - distance, N_X) * rows, 0))
        return whole

    def down_projection(hidden):
        return jnp.dot(hidden, dn, preferred_element_type=F32).astype(BF16)

    far = N_Z // 2
    cut = tok_rows // 2
    mine = jnp.concatenate([tokens, table], axis=1)
    blocks = {0: mine}
    sent, scatters = [], []
    up = down_ = mine
    for step in range(1, far + 1):
        if step > 2 and len(sent) > step - 3:
            up, down_ = after(up, sent[step - 3]), after(down_, sent[step - 3])
        if step < far:
            up, down_ = shift(up, "z", 1), shift(down_, "z", -1)
            blocks[step], blocks[-step] = up, down_
        else:
            blocks[far] = jnp.concatenate([shift(up[:cut], "z", 1), shift(down_[cut:], "z", -1)], axis=0)
        while len(sent) < len(GROUPS) and all(d in blocks for d in GROUPS[len(sent)]):
            outgoing, scatter = pick_rows(blocks, GROUPS[len(sent)])
            sent.append(outgoing)
            scatters.append(scatter)
    pres = [scatter_x(up_projection(cross(outgoing))) for outgoing in sent]
    sums = {}
    back = None
    for group, pre, scatter in zip(GROUPS, pres, scatters):
        result = down_projection(gather_x(activation(pre)))
        if back is not None:
            result = after(result, back)
        back = cross(result)
        summed = lax.dot_general(scatter, back, (((0,), (0,)), ((), ())), preferred_element_type=F32).astype(BF16)
        for i, d in enumerate(group):
            sums[d] = summed[i * tok_rows:(i + 1) * tok_rows]
    width = feat_width // HALVES
    pieces = [
        scatter_z(lambda d: sums[d][:, h * width:(h + 1) * width])
        for h in range(HALVES)
    ]
    return jnp.concatenate(pieces, axis=1)


def solution(mesh):
    grid = Mesh(mesh.devices.reshape(mesh.devices.shape[0], N_Y, N_Z, N_C), ("x", "y", "z", "c"))
    expert = ("y", "z", "c")
    return jax.shard_map(
        body,
        mesh=grid,
        in_specs=(
            P(expert, "x"),
            P(expert, "x", None, None),
            P(expert, None, "x"),
            P(expert, None),
            P(expert, None),
            P(),
        ),
        out_specs=P(expert, "x"),
        check_vma=False,
    )
```

```python
import jax
import jax.numpy as jnp
from jax import lax
from jax.experimental import pallas as pl
from jax.sharding import Mesh, PartitionSpec as P

N_X, N_Y, N_Z, N_C = 4, 4, 8, 2
N_YC = N_Y * N_C
GROUPS = ((0, 1, -1, 2), (-2, 3, -3, 4))
HALVES = 1
RS_SC = False
BF16 = jnp.bfloat16
F32 = jnp.float32


def shift(block, axis, distance):
    size = lax.axis_size(axis)
    return lax.ppermute(block, axis, [(i, (i + distance) % size) for i in range(size)])


def after(value, *others):
    anywhere = pl.BlockSpec(memory_space=pl.ANY)
    return pl.pallas_call(
        lambda *refs: None,
        out_shape=jax.ShapeDtypeStruct(value.shape, value.dtype),
        in_specs=[anywhere] * (1 + len(others)),
        out_specs=anywhere,
        input_output_aliases={0: 0},
        cost_estimate=pl.CostEstimate(flops=0, bytes_accessed=0, transcendentals=0),
        name="after",
    )(value, *others)


def routing_table(route_ids, route_weight, swap_flags):
    tok_rows = route_ids.shape[0]
    experts = swap_flags.shape[0]
    half = experts // 2
    hit = route_ids[:, :, None] == jnp.arange(experts, dtype=jnp.int32)
    named = jnp.any(hit, axis=1).astype(F32)
    weight = jnp.sum(jnp.where(hit, route_weight.astype(F32)[:, :, None], 0.0), axis=1)
    swapped = swap_flags[None, :] == 1
    named = jnp.where(swapped, jnp.roll(named, half, axis=1), named)
    weight = jnp.where(swapped, jnp.roll(weight, half, axis=1), weight)
    upto = jnp.tril(jnp.ones((tok_rows, tok_rows), BF16))
    place = jnp.dot(upto, named.astype(BF16), preferred_element_type=F32) * named
    return jnp.concatenate([place, weight], axis=1).astype(BF16)


def scatter_z(part):
    far = N_Z // 2
    cut = part(far).shape[0] // 2
    down = part(far)[:cut]
    up = part(far)[cut:]
    down, up = shift(down, "z", -1), shift(up, "z", 1)
    down = jnp.concatenate([part(far - 1)[:cut] + down, part(far - 1)[cut:]], axis=0)
    up = jnp.concatenate([part(1 - far)[:cut], part(1 - far)[cut:] + up], axis=0)
    for step in range(far - 2, 0, -1):
        down = part(step) + shift(down, "z", -1)
        up = part(-step) + shift(up, "z", 1)
    mine = part(0).astype(F32) + shift(down, "z", -1).astype(F32) + shift(up, "z", 1).astype(F32)
    return mine.astype(BF16)


def body(tokens, gate_up, down, route_ids, route_weight, swap_flags):
    tok_rows, feat_width = tokens.shape
    experts = swap_flags.shape[0]
    hidden_units = down.shape[1]
    top = route_ids.shape[1]
    capacity = min(tok_rows, 9 * tok_rows * top // (8 * experts))
    flat_gu = gate_up[0].reshape(feat_width, 2 * hidden_units)
    dn = down[0]
    my_x, my_z = lax.axis_index("x"), lax.axis_index("z")

    table = routing_table(route_ids, route_weight, swap_flags)
    dest = jnp.arange(N_YC, dtype=jnp.int32)
    plane = ((dest // N_C) * N_Z + my_z) * N_C + dest % N_C
    pick = (jnp.arange(experts, dtype=jnp.int32)[:, None] == plane[None, :]).astype(BF16)

    def pick_rows(blocks, group):
        count = len(group)
        rows = -(-count * capacity // 8) * 8
        toks = count * tok_rows
        row = jnp.arange(rows, dtype=jnp.int32)
        tok = jnp.arange(toks, dtype=jnp.int32)
        same = (row // capacity)[:, None] == (tok // tok_rows)[None, :]
        want = (row % capacity + 1).astype(F32)
        column = jnp.concatenate([blocks[d] for d in group], axis=0)
        places = jnp.dot(column[:, feat_width:feat_width + experts], pick, preferred_element_type=F32).T
        weights = jnp.dot(column[:, feat_width + experts:], pick, preferred_element_type=F32).T
        chosen = same[None] & (places[:, None, :] == want[None, :, None])
        gather = chosen.astype(BF16).reshape(N_YC * rows, toks)
        scatter = jnp.where(chosen, weights[:, None, :], 0.0).astype(BF16).reshape(N_YC * rows, toks)
        outgoing = jnp.dot(gather, column[:, :feat_width], preferred_element_type=F32).astype(BF16)
        return outgoing, scatter

    def cross(rows):
        blocks = rows.reshape(N_YC, rows.shape[0] // N_YC, feat_width)
        return lax.all_to_all(blocks, ("y", "c"), 0, 0, tiled=True).reshape(rows.shape)

    def up_projection(rows):
        return jnp.dot(rows, flat_gu, preferred_element_type=F32).astype(BF16)

    def scatter_x(partial):
        if RS_SC:
            return lax.psum_scatter(partial, "x", scatter_dimension=0, tiled=True).astype(F32)
        share = partial.shape[0] // N_X
        total = None
        for distance in (2, 1, 3, 0):
            piece = lax.dynamic_slice_in_dim(partial, lax.rem(my_x + distance, N_X) * share, share, axis=0)
            if distance:
                piece = shift(piece, "x", distance)
            total = piece.astype(F32) if total is None else total + piece.astype(F32)
        return total

    def activation(pre):
        return (jax.nn.silu(pre[:, :hidden_units]) * pre[:, hidden_units:]).astype(BF16)

    def gather_x(block):
        rows = block.shape[0]
        whole = jnp.zeros((N_X * rows, hidden_units), BF16)
        for distance in (0, 1, 3, 2):
            piece = shift(block, "x", distance) if distance else block
            whole = lax.dynamic_update_slice(whole, piece, (lax.rem(my_x + N_X - distance, N_X) * rows, 0))
        return whole

    def down_projection(hidden):
        return jnp.dot(hidden, dn, preferred_element_type=F32).astype(BF16)

    far = N_Z // 2
    cut = tok_rows // 2
    mine = jnp.concatenate([tokens, table], axis=1)
    blocks = {0: mine}
    sent, scatters = [], []
    up = down_ = mine
    for step in range(1, far + 1):
        if step > 2 and len(sent) > step - 3:
            up, down_ = after(up, sent[step - 3]), after(down_, sent[step - 3])
        if step < far:
            up, down_ = shift(up, "z", 1), shift(down_, "z", -1)
            blocks[step], blocks[-step] = up, down_
        else:
            blocks[far] = jnp.concatenate([shift(up[:cut], "z", 1), shift(down_[cut:], "z", -1)], axis=0)
        while len(sent) < len(GROUPS) and all(d in blocks for d in GROUPS[len(sent)]):
            outgoing, scatter = pick_rows(blocks, GROUPS[len(sent)])
            sent.append(outgoing)
            scatters.append(scatter)
    pres = [scatter_x(up_projection(cross(outgoing))) for outgoing in sent]
    sums = {}
    back = None
    for group, pre, scatter in zip(GROUPS, pres, scatters):
        result = down_projection(gather_x(activation(pre)))
        if back is not None:
            result = after(result, back)
        back = cross(result)
        summed = lax.dot_general(scatter, back, (((0,), (0,)), ((), ())), preferred_element_type=F32).astype(BF16)
        for i, d in enumerate(group):
            sums[d] = summed[i * tok_rows:(i + 1) * tok_rows]
    width = feat_width // HALVES
    pieces = [
        scatter_z(lambda d: sums[d][:, h * width:(h + 1) * width])
        for h in range(HALVES)
    ]
    return jnp.concatenate(pieces, axis=1)


def solution(mesh):
    grid = Mesh(mesh.devices.reshape(mesh.devices.shape[0], N_Y, N_Z, N_C), ("x", "y", "z", "c"))
    expert = ("y", "z", "c")
    return jax.shard_map(
        body,
        mesh=grid,
        in_specs=(
            P(expert, "x"),
            P(expert, "x", None, None),
            P(expert, None, "x"),
            P(expert, None),
            P(expert, None),
            P(),
        ),
        out_specs=P(expert, "x"),
        check_vma=False,
    )
```

```python
import jax
import jax.numpy as jnp
from jax import lax
from jax.experimental import pallas as pl
from jax.sharding import Mesh, PartitionSpec as P

N_X, N_Y, N_Z, N_C = 4, 4, 8, 2
N_YC = N_Y * N_C
GROUPS = ((0, 1, -1, 2), (-2, 3, -3, 4))
HALVES = 1
RS_SC = False
BF16 = jnp.bfloat16
F32 = jnp.float32


def shift(block, axis, distance):
    size = lax.axis_size(axis)
    return lax.ppermute(block, axis, [(i, (i + distance) % size) for i in range(size)])


def after(value, *others):
    anywhere = pl.BlockSpec(memory_space=pl.ANY)
    return pl.pallas_call(
        lambda *refs: None,
        out_shape=jax.ShapeDtypeStruct(value.shape, value.dtype),
        in_specs=[anywhere] * (1 + len(others)),
        out_specs=anywhere,
        input_output_aliases={0: 0},
        cost_estimate=pl.CostEstimate(flops=0, bytes_accessed=0, transcendentals=0),
        name="after",
    )(value, *others)


def routing_table(route_ids, route_weight, swap_flags):
    tok_rows = route_ids.shape[0]
    experts = swap_flags.shape[0]
    half = experts // 2
    hit = route_ids[:, :, None] == jnp.arange(experts, dtype=jnp.int32)
    named = jnp.any(hit, axis=1).astype(F32)
    weight = jnp.sum(jnp.where(hit, route_weight.astype(F32)[:, :, None], 0.0), axis=1)
    swapped = swap_flags[None, :] == 1
    named = jnp.where(swapped, jnp.roll(named, half, axis=1), named)
    weight = jnp.where(swapped, jnp.roll(weight, half, axis=1), weight)
    upto = jnp.tril(jnp.ones((tok_rows, tok_rows), BF16))
    place = jnp.dot(upto, named.astype(BF16), preferred_element_type=F32) * named
    return jnp.concatenate([place, weight], axis=1).astype(BF16)


def scatter_z(part):
    far = N_Z // 2
    cut = part(far).shape[0] // 2
    down = part(far)[:cut]
    up = part(far)[cut:]
    down, up = shift(down, "z", -1), shift(up, "z", 1)
    down = jnp.concatenate([part(far - 1)[:cut] + down, part(far - 1)[cut:]], axis=0)
    up = jnp.concatenate([part(1 - far)[:cut], part(1 - far)[cut:] + up], axis=0)
    for step in range(far - 2, 0, -1):
        down = part(step) + shift(down, "z", -1)
        up = part(-step) + shift(up, "z", 1)
    mine = part(0).astype(F32) + shift(down, "z", -1).astype(F32) + shift(up, "z", 1).astype(F32)
    return mine.astype(BF16)


def body(tokens, gate_up, down, route_ids, route_weight, swap_flags):
    tok_rows, feat_width = tokens.shape
    experts = swap_flags.shape[0]
    hidden_units = down.shape[1]
    top = route_ids.shape[1]
    capacity = min(tok_rows, 9 * tok_rows * top // (8 * experts))
    flat_gu = gate_up[0].reshape(feat_width, 2 * hidden_units)
    dn = down[0]
    my_x, my_z = lax.axis_index("x"), lax.axis_index("z")

    table = routing_table(route_ids, route_weight, swap_flags)
    dest = jnp.arange(N_YC, dtype=jnp.int32)
    plane = ((dest // N_C) * N_Z + my_z) * N_C + dest % N_C
    pick = (jnp.arange(experts, dtype=jnp.int32)[:, None] == plane[None, :]).astype(BF16)

    def pick_rows(blocks, group):
        count = len(group)
        rows = -(-count * capacity // 8) * 8
        toks = count * tok_rows
        row = jnp.arange(rows, dtype=jnp.int32)
        tok = jnp.arange(toks, dtype=jnp.int32)
        same = (row // capacity)[:, None] == (tok // tok_rows)[None, :]
        want = (row % capacity + 1).astype(F32)
        column = jnp.concatenate([blocks[d] for d in group], axis=0)
        places = jnp.dot(column[:, feat_width:feat_width + experts], pick, preferred_element_type=F32).T
        weights = jnp.dot(column[:, feat_width + experts:], pick, preferred_element_type=F32).T
        chosen = same[None] & (places[:, None, :] == want[None, :, None])
        gather = chosen.astype(BF16).reshape(N_YC * rows, toks)
        scatter = jnp.where(chosen, weights[:, None, :], 0.0).astype(BF16).reshape(N_YC * rows, toks)
        outgoing = jnp.dot(gather, column[:, :feat_width], preferred_element_type=F32).astype(BF16)
        return outgoing, scatter

    def cross(rows):
        blocks = rows.reshape(N_YC, rows.shape[0] // N_YC, feat_width)
        return lax.all_to_all(blocks, ("y", "c"), 0, 0, tiled=True).reshape(rows.shape)

    def up_projection(rows):
        return jnp.dot(rows, flat_gu, preferred_element_type=F32).astype(BF16)

    def scatter_x(partial):
        if RS_SC:
            return lax.psum_scatter(partial, "x", scatter_dimension=0, tiled=True).astype(F32)
        share = partial.shape[0] // N_X
        total = None
        for distance in (2, 1, 3, 0):
            piece = lax.dynamic_slice_in_dim(partial, lax.rem(my_x + distance, N_X) * share, share, axis=0)
            if distance:
                piece = shift(piece, "x", distance)
            total = piece.astype(F32) if total is None else total + piece.astype(F32)
        return total

    def activation(pre):
        return (jax.nn.silu(pre[:, :hidden_units]) * pre[:, hidden_units:]).astype(BF16)

    def gather_x(block):
        rows = block.shape[0]
        whole = jnp.zeros((N_X * rows, hidden_units), BF16)
        for distance in (0, 1, 3, 2):
            piece = shift(block, "x", distance) if distance else block
            whole = lax.dynamic_update_slice(whole, piece, (lax.rem(my_x + N_X - distance, N_X) * rows, 0))
        return whole

    def down_projection(hidden):
        return jnp.dot(hidden, dn, preferred_element_type=F32).astype(BF16)

    far = N_Z // 2
    cut = tok_rows // 2
    mine = jnp.concatenate([tokens, table], axis=1)
    blocks = {0: mine}
    sent, scatters = [], []
    up = down_ = mine
    for step in range(1, far + 1):
        if step > 2 and len(sent) > step - 3:
            up, down_ = after(up, sent[step - 3]), after(down_, sent[step - 3])
        if step < far:
            up, down_ = shift(up, "z", 1), shift(down_, "z", -1)
            blocks[step], blocks[-step] = up, down_
        else:
            blocks[far] = jnp.concatenate([shift(up[:cut], "z", 1), shift(down_[cut:], "z", -1)], axis=0)
        while len(sent) < len(GROUPS) and all(d in blocks for d in GROUPS[len(sent)]):
            outgoing, scatter = pick_rows(blocks, GROUPS[len(sent)])
            sent.append(outgoing)
            scatters.append(scatter)
    pres, partial = [], None
    for outgoing in sent:
        if partial is not None:
            outgoing = after(outgoing, partial)
        partial = up_projection(cross(outgoing))
        pres.append(scatter_x(partial))
    sums = {}
    back = None
    for group, pre, scatter in zip(GROUPS, pres, scatters):
        result = down_projection(gather_x(activation(pre)))
        if back is not None:
            result = after(result, back)
        back = cross(result)
        summed = lax.dot_general(scatter, back, (((0,), (0,)), ((), ())), preferred_element_type=F32).astype(BF16)
        for i, d in enumerate(group):
            sums[d] = summed[i * tok_rows:(i + 1) * tok_rows]
    width = feat_width // HALVES
    pieces = [
        scatter_z(lambda d: sums[d][:, h * width:(h + 1) * width])
        for h in range(HALVES)
    ]
    return jnp.concatenate(pieces, axis=1)


def solution(mesh):
    grid = Mesh(mesh.devices.reshape(mesh.devices.shape[0], N_Y, N_Z, N_C), ("x", "y", "z", "c"))
    expert = ("y", "z", "c")
    return jax.shard_map(
        body,
        mesh=grid,
        in_specs=(
            P(expert, "x"),
            P(expert, "x", None, None),
            P(expert, None, "x"),
            P(expert, None),
            P(expert, None),
            P(),
        ),
        out_specs=P(expert, "x"),
        check_vma=False,
    )
```
